32 devices in a mesh: inst: 2 (over x), section: 2 (over core), tensor: 8 (over z, y).
Axes of the slice: x: 2, y: 2, z: 4, core: 2. Of those that a mesh axis runs over, the one named last changes fastest.
Arguments:
- queries: bfloat16 [2, 2, 8, 6, 1024], P('inst', 'section', 'tensor'), may hold values from -6 to 6
- resident_kv: bfloat16 [2, 2, 8, 2, 6, 2048, 256], P('inst', 'section', 'tensor'), may hold values from -6 to 6
- row_lengths: int32 [2, 6], P('inst'), may hold values from 2 to 2048, as said below
- out_weight: bfloat16 [2, 2, 8, 1024, 4096], P('inst', 'section', 'tensor'), may hold values from -0.5 to 0.5
- outgoing_kv: bfloat16 [2, 2, 8, 2, 256, 16, 256], P('inst', 'section', 'tensor'), may hold values from -6 to 6
- block_order: int32 [2, 2, 8, 256], P('inst', 'section', 'tensor'), may hold values from 0 to 255, each once within a row
- sent_length: int32 [2], P('inst'), may hold values from 1024 to 4096, as said below
Outputs:
- attn_out: float32 [2, 4, 6, 4096], P('inst', 'section', None, 'tensor')
- arrived_kv: bfloat16 [2, 2, 8, 2, 4096, 256], P('inst', 'section', 'tensor')
The draws below stay inside these ranges and needn't reach their ends.
Inputs may be any that keep to these rules, and one draw needn't show every extreme that they name: `row_lengths`: some row of each instance attends 2048 positions. `sent_length`: one of the two instances sends 4096 valid positions, the other fewer. `block_order`: each device's list is a permutation of its 256 stored blocks.
All inputs are finite; a program needn't handle non-finite values.
Results may differ from the reference program's by a relative error of at most 0.005.
Values may be sent and summed in bfloat16 or wider, within the bound.
A program may use at most 128 MiB of HBM per device.

```python
import jax
import jax.numpy as jnp
from jax import lax

D = 4096
HEADS = 32
KV_HEADS = 8
HEAD_DIM = 128
ROWS = 6
CTX = 2048
MIG_LEN = 4096
BLK = 16
NBLK = 256
SLOTS = 8
N_SECTION = 2
N_TENSOR = 8


def draw_resident_kv(key, part):
    key = jax.random.fold_in(key, 11)
    cache_units = jnp.clip(jax.random.normal(key, (2, N_SECTION, N_TENSOR, 2, ROWS, CTX, 2 * HEAD_DIM), jnp.float32), -6.0, 6.0)
    return cache_units.astype(jnp.bfloat16)


def draw_queries(key, part):
    key = jax.random.fold_in(key, 12)
    query_all = jnp.clip(2.0 * jax.random.normal(key, (2, N_SECTION, N_TENSOR, ROWS, SLOTS, HEAD_DIM), jnp.float32), -6.0, 6.0)
    return query_all.reshape(2, N_SECTION, N_TENSOR, ROWS, SLOTS * HEAD_DIM).astype(jnp.bfloat16)


def draw_row_lengths(key, part):
    key = jax.random.fold_in(key, 13)
    length_key, pick_key = jax.random.split(key)
    lengths = jax.random.randint(length_key, (2, ROWS), 2, CTX + 1, dtype=jnp.int32)
    longest = jax.random.randint(pick_key, (2, 1), 0, ROWS, dtype=jnp.int32)
    row_ids = jnp.arange(ROWS, dtype=jnp.int32)[None, :]
    return jnp.where(row_ids == longest, CTX, lengths).astype(jnp.int32)


def draw_sent_length(key, part):
    key = jax.random.fold_in(key, 27)
    length_key, pick_key = jax.random.split(key)
    lengths = jax.random.randint(length_key, (2,), MIG_LEN // 4, MIG_LEN, dtype=jnp.int32)
    longest = jax.random.randint(pick_key, (), 0, 2, dtype=jnp.int32)
    return jnp.where(jnp.arange(2, dtype=jnp.int32) == longest, MIG_LEN, lengths).astype(jnp.int32)


def spiked(result, rng, source, target, blocks, factor):
    def block_of(dim):
        return (jnp.arange(result.shape[dim]) // (result.shape[dim] // blocks)).reshape((-1,) + (1,) * (result.ndim - 1 - dim))

    near = jax.random.permutation(rng, blocks)[block_of(target)]
    other_side = (block_of(target) + blocks // 2) % blocks
    return jnp.where((block_of(source) == near) | (block_of(source) == other_side), factor * result, result)


def levels(rng, dims, cuts, least, top_value):
    factor_of = 1.0
    for axis_at, blocks in cuts:
        heights = jax.random.uniform(jax.random.fold_in(jax.random.fold_in(rng, 6), axis_at), (blocks,), jnp.float32, least / len(cuts), top_value / len(cuts))
        factor_of = factor_of * jnp.repeat(jnp.exp(heights), dims[axis_at] // blocks).reshape((-1,) + (1,) * (len(dims) - 1 - axis_at))
    return factor_of


def gaussian(own_key, dims, spread, most, pieces=(), kind=jnp.bfloat16):
    entries = jax.random.normal(own_key, dims, jnp.float32) * spread
    if len(pieces) > 0:
        entries = levels(own_key, dims, pieces, -0.22, 0.18) * entries
    return jnp.clip(entries, min=-most, max=most).astype(kind)


def noise_with(own_key, dims, width, bound, shards, heavy, held_as=jnp.bfloat16):
    entries = width * jax.random.normal(own_key, dims, jnp.float32)
    if shards:
        entries = entries * levels(own_key, dims, shards, -0.22, 0.18)
    return jnp.clip(spiked(entries, jax.random.fold_in(own_key, 3), *heavy), -bound, bound).astype(held_as)


def setup_inputs(seed: int = 0) -> dict:
    splits = jax.random.split(jax.random.key(seed), 8)
    return {
        "queries": draw_queries(jax.random.fold_in(splits[7], 71), 0),
        "resident_kv": draw_resident_kv(jax.random.fold_in(splits[7], 71), 0),
        "row_lengths": draw_row_lengths(jax.random.fold_in(splits[7], 71), 0),
        "out_weight": noise_with(splits[3], (2, N_SECTION, N_TENSOR, SLOTS * HEAD_DIM, D), (HEADS * HEAD_DIM // 16) ** -0.5, 0.5, ((0, 2), (1, 2), (2, 8)), (2, 4, 8, 2.0)),
        "outgoing_kv": gaussian(splits[4], (2, N_SECTION, N_TENSOR, 2, NBLK, BLK, 2 * HEAD_DIM), 1.0, 6.0, ((0, 2), (1, 2), (2, 8))),
        "block_order": jax.vmap(lambda own: jax.random.permutation(own, NBLK))(jax.random.split(splits[5], 2 * N_SECTION * N_TENSOR)).reshape((2, N_SECTION, N_TENSOR, NBLK)).astype(jnp.int32),
        "sent_length": draw_sent_length(jax.random.fold_in(splits[7], 71), 0),
    }


def ordered_units(outgoing_kv, block_order, sent_length, sender):
    stored = outgoing_kv[sender]
    section_ids = jnp.arange(N_SECTION, dtype=jnp.int32)[:, None, None]
    tensor_ids = jnp.arange(N_TENSOR, dtype=jnp.int32)[None, :, None]
    logical = stored[section_ids, tensor_ids, :, block_order[sender]]
    logical = jnp.transpose(logical, (0, 1, 3, 2, 4, 5))
    logical = logical.reshape(N_SECTION, N_TENSOR, 2, MIG_LEN, 2 * HEAD_DIM)
    positions = jnp.arange(MIG_LEN, dtype=jnp.int32)
    keep_mask = (positions < sent_length[sender])[None, None, None, :, None]
    return jnp.where(keep_mask, logical, jnp.zeros_like(logical))


def receive(logical_first, logical_second):
    tensor_ids = jnp.arange(N_TENSOR, dtype=jnp.int32)
    parity = tensor_ids % 2
    pair_base = tensor_ids - parity
    paired = SLOTS > HEADS // KV_HEADS
    unit_sent = parity if paired else jnp.zeros_like(parity)
    into_second = jnp.stack([logical_first[:, pair_base + unit_pos, unit_sent] for unit_pos in (0, 1)], axis=2)
    if paired:
        into_first = jnp.stack([logical_second[:, pair_base + unit_pos, parity] for unit_pos in (0, 1)], axis=2)
    else:
        kept_unit = logical_second[:, tensor_ids, parity]
        into_first = jnp.stack([kept_unit, jnp.zeros_like(kept_unit)], axis=2)
    return jnp.stack([into_first, into_second])


def attend_device(query_rows, cache_units, lengths, unit_of):
    query_heads = query_rows.astype(jnp.float32).reshape(ROWS, SLOTS, HEAD_DIM)
    key_part = cache_units[..., :HEAD_DIM].astype(jnp.float32)
    value_part = cache_units[..., HEAD_DIM:].astype(jnp.float32)
    scores = jnp.einsum("rkd,urcd->ukrc", query_heads, key_part) * (HEAD_DIM ** -0.5)
    first_unit = (unit_of == 0)[:, None, None]
    chosen = jnp.where(first_unit, scores[0], scores[1])
    live_mask = jnp.arange(CTX, dtype=jnp.int32)[None, :] < lengths[:, None]
    chosen = jnp.where(live_mask[None], chosen, -1e30)
    row_top = jnp.max(chosen, axis=2, keepdims=True)
    raised = jnp.exp(chosen - row_top)
    weights = (raised / jnp.sum(raised, axis=2, keepdims=True)).astype(jnp.bfloat16)
    mixture = jnp.einsum("krc,urcd->ukrd", weights.astype(jnp.float32), value_part)
    head_out = jnp.where(first_unit, mixture[0], mixture[1]).astype(jnp.bfloat16)
    return jnp.transpose(head_out, (1, 0, 2)).reshape(ROWS, SLOTS * HEAD_DIM)


def project_layers(flat_heads, weight, layer_of):
    lane_layer = jnp.repeat(layer_of, HEAD_DIM)
    masked = jnp.stack([jnp.where(lane_layer[None, :] == layer_pos, flat_heads, jnp.zeros_like(flat_heads)) for layer_pos in (0, 1)])
    return jnp.einsum("jrs,sd->jrd", masked.astype(jnp.float32), weight.astype(jnp.float32))


def reference(queries, resident_kv, row_lengths, out_weight, outgoing_kv, block_order, sent_length):
    slot_ids = jnp.arange(SLOTS, dtype=jnp.int32)
    per_layer = SLOTS // 2
    group_size = HEADS // KV_HEADS
    layer_blocks = []
    for inst_pos in range(2):
        section_blocks = []
        for section_pos in range(N_SECTION):
            def device_term(inputs):
                query_rows, cache_units, weight, tensor_pos = inputs
                parity = tensor_pos % 2
                if inst_pos == 1:
                    unit_of = slot_ids // per_layer
                    layer_of = slot_ids // per_layer
                else:
                    unit_of = slot_ids // group_size
                    layer_of = jnp.zeros_like(slot_ids) + parity
                flat_heads = attend_device(query_rows, cache_units, row_lengths[inst_pos], unit_of)
                return project_layers(flat_heads, weight, layer_of)

            device_terms = lax.map(device_term, (queries[inst_pos, section_pos], resident_kv[inst_pos, section_pos], out_weight[inst_pos, section_pos], jnp.arange(N_TENSOR, dtype=jnp.int32)))
            section_blocks.append(jnp.sum(device_terms, axis=0))
        layer_blocks.append(jnp.concatenate(section_blocks, axis=0))
    attn_out = jnp.stack(layer_blocks)
    logical_first = ordered_units(outgoing_kv, block_order, sent_length, 0)
    logical_second = ordered_units(outgoing_kv, block_order, sent_length, 1)
    arrived_kv = receive(logical_first, logical_second)
    return attn_out, arrived_kv
```

```python
import functools

import jax
import jax.numpy as jnp
from jax import lax
from jax.experimental import pallas as pl
from jax.experimental.pallas import tpu as pltpu
from jax.sharding import PartitionSpec as P

HEADS = 32
KV_HEADS = 8
SHARES = (1, 3, 4, 4, 3, 1)


def halved_sum(value, axis):
    size = lax.axis_size(axis)
    place = lax.axis_index(axis)
    bit = size.bit_length() - 2
    while bit >= 0:
        step = 1 << bit
        half = value.shape[-1] // 2
        side = (place // step) % 2
        kept = lax.dynamic_slice_in_dim(value, side * half, half, value.ndim - 1)
        given = lax.dynamic_slice_in_dim(value, (1 - side) * half, half, value.ndim - 1)
        value = kept + lax.ppermute(given, axis, [(i, i ^ step) for i in range(size)])
        bit -= 1
    return value


def sent_units(paired):
    parity = lax.axis_index("tensor") % 2
    if paired:
        return parity, 1 - parity
    return lax.axis_index("inst") * parity, 0 * parity


def order_kernel(starts, paired, order_ref, length_ref, stored_ref, *rest):
    chunk_refs, (edge, blank, edge_sem, sem) = rest[:-4], rest[-4:]
    block_len = edge.shape[1]
    units = sent_units(paired)
    length = length_ref[0]
    full = length // block_len
    blank[...] = jnp.zeros_like(blank)

    for part, start in enumerate(starts):
        count = chunk_refs[2 * part].shape[0] // block_len
        whole = jnp.clip(full - start, 0, count)

        def copy_block(i, carry):
            stored_at = order_ref[start + i]
            for way in range(2):
                pltpu.make_async_copy(
                    stored_ref.at[units[way], stored_at],
                    chunk_refs[2 * part + way].at[pl.ds(i * block_len, block_len)],
                    sem,
                ).start()
            return carry

        def blank_block(i, carry):
            for way in range(2):
                pltpu.make_async_copy(
                    blank, chunk_refs[2 * part + way].at[pl.ds(i * block_len, block_len)], sem
                ).start()
            return carry

        lax.fori_loop(0, whole, copy_block, 0)
        here = (full >= start) & (full < start + count)

        @pl.when(here)
        def _():
            stored_at = order_ref[full]
            for way in range(2):
                fetch = pltpu.make_async_copy(
                    stored_ref.at[units[way], stored_at], edge.at[way], edge_sem
                )
                fetch.start()
                fetch.wait()
            rows = lax.broadcasted_iota(jnp.int32, edge.shape, 1)
            edge[...] = jnp.where(
                rows < length - full * block_len, edge[...].astype(jnp.float32), 0.0
            ).astype(edge.dtype)
            for way in range(2):
                pltpu.make_async_copy(
                    edge.at[way],
                    chunk_refs[2 * part + way].at[pl.ds((full - start) * block_len, block_len)],
                    sem,
                ).start()

        lax.fori_loop(whole + here.astype(jnp.int32), count, blank_block, 0)

    for chunk_ref in chunk_refs:
        pltpu.make_async_copy(chunk_ref, chunk_ref, sem).wait()


def first_kernel(paired, order_ref, stored_ref, same_ref, other_ref, sem):
    block_len = stored_ref.shape[2]
    units = sent_units(paired)
    for i in range(same_ref.shape[0] // block_len):
        for unit, chunk_ref in zip(units, (same_ref, other_ref)):
            pltpu.make_async_copy(
                stored_ref.at[unit, order_ref[i]], chunk_ref.at[pl.ds(i * block_len, block_len)], sem
            ).start()
    for chunk_ref in (same_ref, other_ref):
        pltpu.make_async_copy(chunk_ref, chunk_ref, sem).wait()


def first_chunks(stored, block_ids, paired, count):
    block_len, lane_width = stored.shape[2:]
    chunk_shape = jax.ShapeDtypeStruct((count * block_len, lane_width), stored.dtype)
    return pl.pallas_call(
        functools.partial(first_kernel, paired),
        out_shape=[chunk_shape] * 2,
        in_specs=[
            pl.BlockSpec(memory_space=pltpu.SMEM),
            pl.BlockSpec(memory_space=pltpu.HBM),
        ],
        out_specs=[pl.BlockSpec(memory_space=pltpu.HBM)] * 2,
        scratch_shapes=[pltpu.SemaphoreType.DMA],
        compiler_params=pltpu.CompilerParams(vmem_limit_bytes=60 * 1024 * 1024),
    )(block_ids, stored)


def room_kernel(out_ref):
    pass


def room(shape, dtype):
    return pl.pallas_call(
        room_kernel,
        out_shape=jax.ShapeDtypeStruct(shape, dtype),
        out_specs=pl.BlockSpec(memory_space=pltpu.HBM),
    )()


def ordered_chunks(stored, block_ids, sent_length, paired, starts, counts):
    block_len, lane_width = stored.shape[2:]
    chunk_shapes = []
    for count in counts:
        chunk_shapes += [jax.ShapeDtypeStruct((count * block_len, lane_width), stored.dtype)] * 2
    total = sum(counts) * block_len * lane_width * 2
    return pl.pallas_call(
        functools.partial(order_kernel, starts, paired),
        out_shape=chunk_shapes,
        in_specs=[
            pl.BlockSpec(memory_space=pltpu.SMEM),
            pl.BlockSpec(memory_space=pltpu.SMEM),
            pl.BlockSpec(memory_space=pltpu.HBM),
        ],
        out_specs=[pl.BlockSpec(memory_space=pltpu.HBM)] * len(chunk_shapes),
        scratch_shapes=[
            pltpu.VMEM((2, block_len, lane_width), stored.dtype),
            pltpu.VMEM((block_len, lane_width), stored.dtype),
            pltpu.SemaphoreType.DMA,
            pltpu.SemaphoreType.DMA,
        ],
        compiler_params=pltpu.CompilerParams(vmem_limit_bytes=48 * 1024 * 1024),
        cost_estimate=pl.CostEstimate(flops=0, bytes_accessed=4 * total, transcendentals=0),
    )(block_ids, sent_length, stored)


def cuts(block_count):
    unit = block_count // 16
    counts = [share * unit for share in SHARES]
    starts = [sum(counts[:i]) for i in range(len(counts))]
    return starts, counts


def crossed(chunk, flip, both):
    size = lax.axis_size("tensor")
    route = [(t, size + (t ^ flip)) for t in range(size)]
    if both:
        route += [(size + t, t ^ flip) for t in range(size)]
    return lax.ppermute(chunk, ("inst", "tensor"), route)


def attend_kernel(group_size, lengths_ref, query_ref, keys_ref, values_ref, out_ref):
    unit, row = pl.program_id(0), pl.program_id(1)
    slot_count, head_dim = query_ref.shape[1:]
    context = keys_ref.shape[0]
    scores = lax.dot_general(
        query_ref[row], keys_ref[...], (((1,), (1,)), ((), ())), preferred_element_type=jnp.float32
    ) * head_dim ** (-0.5)
    positions = lax.broadcasted_iota(jnp.int32, (slot_count, context), 1)
    scores = jnp.where(positions < lengths_ref[0, row], scores, -1e30)
    raised = jnp.exp(scores - jnp.max(scores, axis=1, keepdims=True))
    weights = (raised / jnp.sum(raised, axis=1, keepdims=True)).astype(jnp.bfloat16)
    mixture = jnp.dot(weights, values_ref[...], preferred_element_type=jnp.float32)
    slot_ids = lax.broadcasted_iota(jnp.int32, (slot_count, head_dim), 0)
    second = lax.axis_index("inst") == 1
    beyond = jnp.where(second, slot_count // 2, group_size)
    mine = (slot_ids >= beyond) == (unit == 1)

    @pl.when(unit == 0)
    def _():
        out_ref[row] = mixture

    @pl.when(unit == 1)
    def _():
        out_ref[row] = jnp.where(mine, mixture, out_ref[row])


def attend_slots(query_rows, cache_units, lengths):
    row_count = query_rows.shape[0]
    unit_count, _, context, lane_width = cache_units.shape
    head_dim = lane_width // 2
    slot_count = query_rows.shape[1] // head_dim
    query_heads = query_rows.reshape(row_count, slot_count, head_dim)
    mixture = pl.pallas_call(
        functools.partial(attend_kernel, HEADS // KV_HEADS),
        grid=(unit_count, row_count),
        out_shape=jax.ShapeDtypeStruct((row_count, slot_count, head_dim), jnp.float32),
        in_specs=[
            pl.BlockSpec(memory_space=pltpu.SMEM),
            pl.BlockSpec((row_count, slot_count, head_dim), lambda u, r: (0, 0, 0)),
            pl.BlockSpec((None, None, context, head_dim), lambda u, r: (u, r, 0, 0)),
            pl.BlockSpec((None, None, context, head_dim), lambda u, r: (u, r, 0, 1)),
        ],
        out_specs=pl.BlockSpec((row_count, slot_count, head_dim), lambda u, r: (0, 0, 0)),
        cost_estimate=pl.CostEstimate(
            flops=4 * cache_units.size * slot_count // 2,
            bytes_accessed=2 * cache_units.size,
            transcendentals=unit_count * row_count * slot_count * context,
        ),
        compiler_params=pltpu.CompilerParams(vmem_limit_bytes=32 * 1024 * 1024),
    )(lengths, query_heads, cache_units, cache_units)
    return mixture.astype(jnp.bfloat16).reshape(row_count, slot_count * head_dim)


def project_layers(flat_heads, weight, layer_of, head_dim):
    lane_layer = jnp.repeat(layer_of, head_dim)
    blank = jnp.zeros_like(flat_heads)
    masked = jnp.stack(
        [jnp.where(lane_layer[None, :] == layer_pos, flat_heads, blank) for layer_pos in (0, 1)]
    )
    return jnp.einsum("jrs,sd->jrd", masked, weight, preferred_element_type=jnp.float32)


def per_device(
    queries, resident_kv, row_lengths, out_weight, outgoing_kv, block_order, sent_length
):
    second = lax.axis_index("inst") == 1
    parity = lax.axis_index("tensor") % 2
    query_rows = queries[0, 0, 0]
    cache_units = resident_kv[0, 0, 0]
    head_dim = cache_units.shape[-1] // 2
    slot_count = query_rows.shape[1] // head_dim
    per_layer = slot_count // 2
    group_size = HEADS // KV_HEADS
    paired = slot_count > group_size
    slot_ids = jnp.arange(slot_count, dtype=jnp.int32)
    layer_of = jnp.where(second, slot_ids // per_layer, parity)
    stored = outgoing_kv[0, 0, 0]
    unit_count, block_count, block_len, lane_width = stored.shape
    block_ids = block_order[0, 0, 0]
    starts, counts = cuts(block_count)
    chunks = list(first_chunks(stored, block_ids, paired, counts[0]))
    chunks += ordered_chunks(stored, block_ids, sent_length, paired, starts[1:], counts[1:])
    if paired:
        same_slot, other_slot = parity, 1 - parity
    else:
        same_slot = jnp.where(second, parity, 0)
        other_slot = jnp.where(second, 1 - parity, 1)
    arrived = room((unit_count, block_count * block_len, lane_width), stored.dtype)
    landed = [None] * len(chunks)

    def send(parts):
        for part in parts:
            landed[2 * part] = crossed(chunks[2 * part], 0, True)
            landed[2 * part + 1] = crossed(chunks[2 * part + 1], 1, paired)

    early = len(counts) - 2
    send(range(early))
    query_rows, cache_units, landed[2], landed[3] = lax.optimization_barrier(
        (query_rows, cache_units, landed[2], landed[3])
    )
    flat_heads = attend_slots(query_rows, cache_units, row_lengths)
    partial_value = project_layers(flat_heads, out_weight[0, 0, 0], layer_of, head_dim)
    totals = halved_sum(partial_value, "tensor")
    totals, *chunks[2 * early :] = lax.optimization_barrier((totals, *chunks[2 * early :]))
    send(range(early, len(counts)))
    for part, start in enumerate(starts):
        for way, slot in enumerate((same_slot, other_slot)):
            place = (slot, start * block_len, 0)
            arrived = lax.dynamic_update_slice(arrived, landed[2 * part + way][None], place)
    return (totals[None], arrived[None, None, None])


def solution(mesh):
    placed = (
        P("inst", "section", "tensor", None, None),
        P("inst", "section", "tensor", None, None, None, None),
        P("inst", None),
        P("inst", "section", "tensor", None, None),
        P("inst", "section", "tensor", None, None, None, None),
        P("inst", "section", "tensor", None),
        P("inst"),
    )
    return jax.shard_map(
        per_device,
        mesh=mesh,
        in_specs=placed,
        out_specs=(
            P("inst", "section", None, "tensor"),
            P("inst", "section", "tensor", None, None, None),
        ),
        check_vma=False,
    )
```

```python
import functools

import jax
import jax.numpy as jnp
from jax import lax
from jax.experimental import pallas as pl
from jax.experimental.pallas import tpu as pltpu
from jax.sharding import PartitionSpec as P

HEADS = 32
KV_HEADS = 8
SHARES = (3, 6, 8, 8, 6, 1)


def halved_sum(value, axis):
    size = lax.axis_size(axis)
    place = lax.axis_index(axis)
    bit = size.bit_length() - 2
    while bit >= 0:
        step = 1 << bit
        half = value.shape[-1] // 2
        side = (place // step) % 2
        kept = lax.dynamic_slice_in_dim(value, side * half, half, value.ndim - 1)
        given = lax.dynamic_slice_in_dim(value, (1 - side) * half, half, value.ndim - 1)
        value = kept + lax.ppermute(given, axis, [(i, i ^ step) for i in range(size)])
        bit -= 1
    return value


def sent_units(paired):
    parity = lax.axis_index("tensor") % 2
    if paired:
        return parity, 1 - parity
    return lax.axis_index("inst") * parity, 0 * parity


def order_kernel(starts, paired, order_ref, length_ref, stored_ref, *rest):
    chunk_refs, (held, edge, blank, edge_sem, sem) = rest[:-5], rest[-5:]
    block_len = edge.shape[1]
    units = sent_units(paired)
    fetches = []
    for way in range(2):
        fetches.append(
            pltpu.make_async_copy(stored_ref.at[units[way]], held.at[way], edge_sem.at[way])
        )
        fetches[way].start()
    length = length_ref[0]
    full = length // block_len
    blank[...] = jnp.zeros_like(blank)
    for fetch in fetches:
        fetch.wait()

    for part, start in enumerate(starts):
        count = chunk_refs[2 * part].shape[0] // block_len
        whole = jnp.clip(full - start, 0, count)

        def copy_block(i, carry):
            stored_at = order_ref[start + i]
            for way in range(2):
                pltpu.make_async_copy(
                    held.at[way, stored_at],
                    chunk_refs[2 * part + way].at[pl.ds(i * block_len, block_len)],
                    sem,
                ).start()
            return carry

        def blank_block(i, carry):
            for way in range(2):
                pltpu.make_async_copy(
                    blank, chunk_refs[2 * part + way].at[pl.ds(i * block_len, block_len)], sem
                ).start()
            return carry

        lax.fori_loop(0, whole, copy_block, 0)
        here = (full >= start) & (full < start + count)

        @pl.when(here)
        def _():
            stored_at = order_ref[full]
            rows = lax.broadcasted_iota(jnp.int32, edge.shape, 1)
            edge[...] = jnp.where(
                rows < length - full * block_len, held[:, stored_at].astype(jnp.float32), 0.0
            ).astype(edge.dtype)
            for way in range(2):
                pltpu.make_async_copy(
                    edge.at[way],
                    chunk_refs[2 * part + way].at[pl.ds((full - start) * block_len, block_len)],
                    sem,
                ).start()

        lax.fori_loop(whole + here.astype(jnp.int32), count, blank_block, 0)

    for chunk_ref in chunk_refs:
        pltpu.make_async_copy(chunk_ref, chunk_ref, sem).wait()


def first_kernel(paired, order_ref, stored_ref, same_ref, other_ref, sem):
    block_len = stored_ref.shape[2]
    units = sent_units(paired)
    for i in range(same_ref.shape[0] // block_len):
        for unit, chunk_ref in zip(units, (same_ref, other_ref)):
            pltpu.make_async_copy(
                stored_ref.at[unit, order_ref[i]], chunk_ref.at[pl.ds(i * block_len, block_len)], sem
            ).start()
    for chunk_ref in (same_ref, other_ref):
        pltpu.make_async_copy(chunk_ref, chunk_ref, sem).wait()


def first_chunks(stored, block_ids, paired, count):
    block_len, lane_width = stored.shape[2:]
    chunk_shape = jax.ShapeDtypeStruct((count * block_len, lane_width), stored.dtype)
    return pl.pallas_call(
        functools.partial(first_kernel, paired),
        out_shape=[chunk_shape] * 2,
        in_specs=[
            pl.BlockSpec(memory_space=pltpu.SMEM),
            pl.BlockSpec(memory_space=pltpu.HBM),
        ],
        out_specs=[pl.BlockSpec(memory_space=pltpu.VMEM)] * 2,
        scratch_shapes=[pltpu.SemaphoreType.DMA],
        compiler_params=pltpu.CompilerParams(vmem_limit_bytes=60 * 1024 * 1024),
    )(block_ids, stored)


def room_kernel(out_ref):
    pass


def room(shape, dtype):
    return pl.pallas_call(
        room_kernel,
        out_shape=jax.ShapeDtypeStruct(shape, dtype),
        out_specs=pl.BlockSpec(memory_space=pltpu.HBM),
    )()


def ordered_chunks(stored, block_ids, sent_length, paired, starts, counts):
    block_len, lane_width = stored.shape[2:]
    chunk_shapes = []
    for count in counts:
        chunk_shapes += [jax.ShapeDtypeStruct((count * block_len, lane_width), stored.dtype)] * 2
    total = sum(counts) * block_len * lane_width * 2
    return pl.pallas_call(
        functools.partial(order_kernel, starts, paired),
        out_shape=chunk_shapes,
        in_specs=[
            pl.BlockSpec(memory_space=pltpu.SMEM),
            pl.BlockSpec(memory_space=pltpu.SMEM),
            pl.BlockSpec(memory_space=pltpu.HBM),
        ],
        out_specs=[pl.BlockSpec(memory_space=pltpu.HBM)] * len(chunk_shapes),
        scratch_shapes=[
            pltpu.VMEM((2,) + stored.shape[1:], stored.dtype),
            pltpu.VMEM((2, block_len, lane_width), stored.dtype),
            pltpu.VMEM((block_len, lane_width), stored.dtype),
            pltpu.SemaphoreType.DMA((2,)),
            pltpu.SemaphoreType.DMA,
        ],
        compiler_params=pltpu.CompilerParams(vmem_limit_bytes=48 * 1024 * 1024),
        cost_estimate=pl.CostEstimate(flops=0, bytes_accessed=4 * total, transcendentals=0),
    )(block_ids, sent_length, stored)


def cuts(block_count):
    unit = block_count // 32
    counts = [share * unit for share in SHARES]
    starts = [sum(counts[:i]) for i in range(len(counts))]
    return starts, counts


def crossed(chunk, flip, both):
    size = lax.axis_size("tensor")
    route = [(t, size + (t ^ flip)) for t in range(size)]
    if both:
        route += [(size + t, t ^ flip) for t in range(size)]
    return lax.ppermute(chunk, ("inst", "tensor"), route)


def attend_kernel(group_size, lengths_ref, query_ref, keys_ref, values_ref, out_ref):
    unit, row = pl.program_id(0), pl.program_id(1)
    slot_count, head_dim = query_ref.shape[1:]
    context = keys_ref.shape[0]
    scores = lax.dot_general(
        query_ref[row], keys_ref[...], (((1,), (1,)), ((), ())), preferred_element_type=jnp.float32
    ) * head_dim ** (-0.5)
    positions = lax.broadcasted_iota(jnp.int32, (slot_count, context), 1)
    scores = jnp.where(positions < lengths_ref[0, row], scores, -1e30)
    raised = jnp.exp(scores - jnp.max(scores, axis=1, keepdims=True))
    weights = (raised / jnp.sum(raised, axis=1, keepdims=True)).astype(jnp.bfloat16)
    mixture = jnp.dot(weights, values_ref[...], preferred_element_type=jnp.float32)
    slot_ids = lax.broadcasted_iota(jnp.int32, (slot_count, head_dim), 0)
    second = lax.axis_index("inst") == 1
    beyond = jnp.where(second, slot_count // 2, group_size)
    mine = (slot_ids >= beyond) == (unit == 1)

    @pl.when(unit == 0)
    def _():
        out_ref[row] = mixture

    @pl.when(unit == 1)
    def _():
        out_ref[row] = jnp.where(mine, mixture, out_ref[row])


def attend_slots(query_rows, cache_units, lengths):
    row_count = query_rows.shape[0]
    unit_count, _, context, lane_width = cache_units.shape
    head_dim = lane_width // 2
    slot_count = query_rows.shape[1] // head_dim
    query_heads = query_rows.reshape(row_count, slot_count, head_dim)
    mixture = pl.pallas_call(
        functools.partial(attend_kernel, HEADS // KV_HEADS),
        grid=(unit_count, row_count),
        out_shape=jax.ShapeDtypeStruct((row_count, slot_count, head_dim), jnp.float32),
        in_specs=[
            pl.BlockSpec(memory_space=pltpu.SMEM),
            pl.BlockSpec((row_count, slot_count, head_dim), lambda u, r: (0, 0, 0)),
            pl.BlockSpec((None, None, context, head_dim), lambda u, r: (u, r, 0, 0)),
            pl.BlockSpec((None, None, context, head_dim), lambda u, r: (u, r, 0, 1)),
        ],
        out_specs=pl.BlockSpec((row_count, slot_count, head_dim), lambda u, r: (0, 0, 0)),
        cost_estimate=pl.CostEstimate(
            flops=4 * cache_units.size * slot_count // 2,
            bytes_accessed=2 * cache_units.size,
            transcendentals=unit_count * row_count * slot_count * context,
        ),
        compiler_params=pltpu.CompilerParams(vmem_limit_bytes=32 * 1024 * 1024),
    )(lengths, query_heads, cache_units, cache_units)
    return mixture.astype(jnp.bfloat16).reshape(row_count, slot_count * head_dim)


def project_layers(flat_heads, weight, layer_of, head_dim):
    lane_layer = jnp.repeat(layer_of, head_dim)
    blank = jnp.zeros_like(flat_heads)
    masked = jnp.stack(
        [jnp.where(lane_layer[None, :] == layer_pos, flat_heads, blank) for layer_pos in (0, 1)]
    )
    return jnp.einsum("jrs,sd->jrd", masked, weight, preferred_element_type=jnp.float32)


def per_device(
    queries, resident_kv, row_lengths, out_weight, outgoing_kv, block_order, sent_length
):
    second = lax.axis_index("inst") == 1
    parity = lax.axis_index("tensor") % 2
    query_rows = queries[0, 0, 0]
    cache_units = resident_kv[0, 0, 0]
    head_dim = cache_units.shape[-1] // 2
    slot_count = query_rows.shape[1] // head_dim
    per_layer = slot_count // 2
    group_size = HEADS // KV_HEADS
    paired = slot_count > group_size
    slot_ids = jnp.arange(slot_count, dtype=jnp.int32)
    layer_of = jnp.where(second, slot_ids // per_layer, parity)
    stored = outgoing_kv[0, 0, 0]
    unit_count, block_count, block_len, lane_width = stored.shape
    block_ids = block_order[0, 0, 0]
    starts, counts = cuts(block_count)
    chunks = list(first_chunks(stored, block_ids, paired, counts[0]))
    chunks += ordered_chunks(stored, block_ids, sent_length, paired, starts[1:], counts[1:])
    if paired:
        same_slot, other_slot = parity, 1 - parity
    else:
        same_slot = jnp.where(second, parity, 0)
        other_slot = jnp.where(second, 1 - parity, 1)
    arrived = room((unit_count, block_count * block_len, lane_width), stored.dtype)
    landed = [None] * len(chunks)

    def send(parts):
        for part in parts:
            landed[2 * part] = crossed(chunks[2 * part], 0, True)
            landed[2 * part + 1] = crossed(chunks[2 * part + 1], 1, paired)

    early = len(counts) - 2
    send(range(early))
    query_rows, cache_units, landed[2], landed[3] = lax.optimization_barrier(
        (query_rows, cache_units, landed[2], landed[3])
    )
    flat_heads = attend_slots(query_rows, cache_units, row_lengths)
    partial_value = project_layers(flat_heads, out_weight[0, 0, 0], layer_of, head_dim)
    totals = halved_sum(partial_value, "tensor")
    totals, *chunks[2 * early :] = lax.optimization_barrier((totals, *chunks[2 * early :]))
    send(range(early, len(counts)))
    for part, start in enumerate(starts):
        for way, slot in enumerate((same_slot, other_slot)):
            place = (slot, start * block_len, 0)
            arrived = lax.dynamic_update_slice(arrived, landed[2 * part + way][None], place)
    return (totals[None], arrived[None, None, None])


def solution(mesh):
    placed = (
        P("inst", "section", "tensor", None, None),
        P("inst", "section", "tensor", None, None, None, None),
        P("inst", None),
        P("inst", "section", "tensor", None, None),
        P("inst", "section", "tensor", None, None, None, None),
        P("inst", "section", "tensor", None),
        P("inst"),
    )
    return jax.shard_map(
        per_device,
        mesh=mesh,
        in_specs=placed,
        out_specs=(
            P("inst", "section", None, "tensor"),
            P("inst", "section", "tensor", None, None, None),
        ),
        check_vma=False,
    )
```

```python
import functools

import jax
import jax.numpy as jnp
from jax import lax
from jax.experimental import pallas as pl
from jax.experimental.pallas import tpu as pltpu
from jax.sharding import PartitionSpec as P

HEADS = 32
KV_HEADS = 8
SHARES = (3, 6, 8, 9, 5, 1)


def halved_sum(value, axis):
    size = lax.axis_size(axis)
    place = lax.axis_index(axis)
    bit = size.bit_length() - 2
    while bit >= 0:
        step = 1 << bit
        half = value.shape[-1] // 2
        side = (place // step) % 2
        kept = lax.dynamic_slice_in_dim(value, side * half, half, value.ndim - 1)
        given = lax.dynamic_slice_in_dim(value, (1 - side) * half, half, value.ndim - 1)
        value = kept + lax.ppermute(given, axis, [(i, i ^ step) for i in range(size)])
        bit -= 1
    return value


def sent_units(paired):
    parity = lax.axis_index("tensor") % 2
    if paired:
        return parity, 1 - parity
    return lax.axis_index("inst") * parity, 0 * parity


def order_kernel(starts, paired, order_ref, length_ref, stored_ref, *rest):
    chunk_refs, (held, edge, blank, edge_sem, sem) = rest[:-5], rest[-5:]
    block_len = edge.shape[1]
    units = sent_units(paired)
    pieces = 8
    span = held.shape[1] // pieces
    for piece in range(pieces):
        for way in range(2):
            here = pl.ds(piece * span, span)
            pltpu.make_async_copy(
                stored_ref.at[units[way], here], held.at[way, here], edge_sem
            ).start()
    length = length_ref[0]
    full = length // block_len
    blank[...] = jnp.zeros_like(blank)
    pltpu.make_async_copy(held, held, edge_sem).wait()

    for part, start in enumerate(starts):
        count = chunk_refs[2 * part].shape[0] // block_len
        whole = jnp.clip(full - start, 0, count)

        def copy_block(i, carry):
            stored_at = order_ref[start + i]
            for way in range(2):
                pltpu.make_async_copy(
                    held.at[way, stored_at],
                    chunk_refs[2 * part + way].at[pl.ds(i * block_len, block_len)],
                    sem,
                ).start()
            return carry

        def blank_block(i, carry):
            for way in range(2):
                pltpu.make_async_copy(
                    blank, chunk_refs[2 * part + way].at[pl.ds(i * block_len, block_len)], sem
                ).start()
            return carry

        lax.fori_loop(0, whole, copy_block, 0)
        here = (full >= start) & (full < start + count)

        @pl.when(here)
        def _():
            stored_at = order_ref[full]
            rows = lax.broadcasted_iota(jnp.int32, edge.shape, 1)
            edge[...] = jnp.where(
                rows < length - full * block_len, held[:, stored_at].astype(jnp.float32), 0.0
            ).astype(edge.dtype)
            for way in range(2):
                pltpu.make_async_copy(
                    edge.at[way],
                    chunk_refs[2 * part + way].at[pl.ds((full - start) * block_len, block_len)],
                    sem,
                ).start()

        lax.fori_loop(whole + here.astype(jnp.int32), count, blank_block, 0)

    for chunk_ref in chunk_refs:
        pltpu.make_async_copy(chunk_ref, chunk_ref, sem).wait()


def first_kernel(start, paired, order_ref, stored_ref, same_ref, other_ref, sem):
    block_len = stored_ref.shape[2]
    units = sent_units(paired)
    for i in range(same_ref.shape[0] // block_len):
        for unit, chunk_ref in zip(units, (same_ref, other_ref)):
            pltpu.make_async_copy(
                stored_ref.at[unit, order_ref[start + i]], chunk_ref.at[pl.ds(i * block_len, block_len)], sem
            ).start()
    for chunk_ref in (same_ref, other_ref):
        pltpu.make_async_copy(chunk_ref, chunk_ref, sem).wait()


def first_chunks(stored, block_ids, paired, start, count):
    block_len, lane_width = stored.shape[2:]
    chunk_shape = jax.ShapeDtypeStruct((count * block_len, lane_width), stored.dtype)
    return pl.pallas_call(
        functools.partial(first_kernel, start, paired),
        out_shape=[chunk_shape] * 2,
        in_specs=[
            pl.BlockSpec(memory_space=pltpu.SMEM),
            pl.BlockSpec(memory_space=pltpu.HBM),
        ],
        out_specs=[pl.BlockSpec(memory_space=pltpu.VMEM)] * 2,
        scratch_shapes=[pltpu.SemaphoreType.DMA],
        compiler_params=pltpu.CompilerParams(vmem_limit_bytes=60 * 1024 * 1024),
    )(block_ids, stored)


def room_kernel(out_ref):
    pass


def room(shape, dtype):
    return pl.pallas_call(
        room_kernel,
        out_shape=jax.ShapeDtypeStruct(shape, dtype),
        out_specs=pl.BlockSpec(memory_space=pltpu.HBM),
    )()


def ordered_chunks(stored, block_ids, sent_length, paired, starts, counts):
    block_len, lane_width = stored.shape[2:]
    chunk_shapes = []
    for count in counts:
        chunk_shapes += [jax.ShapeDtypeStruct((count * block_len, lane_width), stored.dtype)] * 2
    total = sum(counts) * block_len * lane_width * 2
    return pl.pallas_call(
        functools.partial(order_kernel, starts, paired),
        out_shape=chunk_shapes,
        in_specs=[
            pl.BlockSpec(memory_space=pltpu.SMEM),
            pl.BlockSpec(memory_space=pltpu.SMEM),
            pl.BlockSpec(memory_space=pltpu.HBM),
        ],
        out_specs=[pl.BlockSpec(memory_space=pltpu.HBM)] * len(chunk_shapes),
        scratch_shapes=[
            pltpu.VMEM((2,) + stored.shape[1:], stored.dtype),
            pltpu.VMEM((2, block_len, lane_width), stored.dtype),
            pltpu.VMEM((block_len, lane_width), stored.dtype),
            pltpu.SemaphoreType.DMA,
            pltpu.SemaphoreType.DMA,
        ],
        compiler_params=pltpu.CompilerParams(vmem_limit_bytes=48 * 1024 * 1024),
        cost_estimate=pl.CostEstimate(flops=0, bytes_accessed=4 * total, transcendentals=0),
    )(block_ids, sent_length, stored)


def place_kernel(starts, slot_of, arrived_ref, *rest):
    landed_refs, (out_ref, sems) = rest[:-2], rest[-2:]
    slots = slot_of()
    copies = []
    for at, (landed_ref, (start, way)) in enumerate(zip(landed_refs, starts)):
        copies.append(
            pltpu.make_async_copy(
                landed_ref, out_ref.at[slots[way], pl.ds(start, landed_ref.shape[0])], sems.at[at]
            )
        )
    for copy in copies:
        copy.start()
    for copy in copies:
        copy.wait()


def place_last(arrived, pieces, starts, paired):
    return pl.pallas_call(
        functools.partial(place_kernel, starts, functools.partial(landing_slots, paired)),
        out_shape=jax.ShapeDtypeStruct(arrived.shape, arrived.dtype),
        in_specs=[pl.BlockSpec(memory_space=pltpu.HBM)] + [pl.BlockSpec(memory_space=pl.ANY)] * len(pieces),
        out_specs=pl.BlockSpec(memory_space=pltpu.HBM),
        scratch_shapes=[pltpu.SemaphoreType.DMA((len(pieces),))],
        input_output_aliases={0: 0},
    )(arrived, *pieces)


def landing_slots(paired):
    parity = lax.axis_index("tensor") % 2
    if paired:
        return parity, 1 - parity
    second = lax.axis_index("inst")
    return second * parity, 1 - second * parity


def cuts(block_count):
    unit = block_count // 32
    counts = [share * unit for share in SHARES]
    starts = [sum(counts[:i]) for i in range(len(counts))]
    return starts, counts


def crossed(chunk, flip, both):
    size = lax.axis_size("tensor")
    route = [(t, size + (t ^ flip)) for t in range(size)]
    if both:
        route += [(size + t, t ^ flip) for t in range(size)]
    return lax.ppermute(chunk, ("inst", "tensor"), route)


def attend_kernel(group_size, lengths_ref, query_ref, keys_ref, values_ref, out_ref):
    unit, row = pl.program_id(0), pl.program_id(1)
    slot_count, head_dim = query_ref.shape[1:]
    context = keys_ref.shape[0]
    scores = lax.dot_general(
        query_ref[row], keys_ref[...], (((1,), (1,)), ((), ())), preferred_element_type=jnp.float32
    ) * head_dim ** (-0.5)
    positions = lax.broadcasted_iota(jnp.int32, (slot_count, context), 1)
    scores = jnp.where(positions < lengths_ref[0, row], scores, -1e30)
    raised = jnp.exp(scores - jnp.max(scores, axis=1, keepdims=True))
    weights = (raised / jnp.sum(raised, axis=1, keepdims=True)).astype(jnp.bfloat16)
    mixture = jnp.dot(weights, values_ref[...], preferred_element_type=jnp.float32)
    slot_ids = lax.broadcasted_iota(jnp.int32, (slot_count, head_dim), 0)
    second = lax.axis_index("inst") == 1
    beyond = jnp.where(second, slot_count // 2, group_size)
    mine = (slot_ids >= beyond) == (unit == 1)

    @pl.when(unit == 0)
    def _():
        out_ref[row] = mixture

    @pl.when(unit == 1)
    def _():
        out_ref[row] = jnp.where(mine, mixture, out_ref[row])


def attend_slots(query_rows, cache_units, lengths):
    row_count = query_rows.shape[0]
    unit_count, _, context, lane_width = cache_units.shape
    head_dim = lane_width // 2
    slot_count = query_rows.shape[1] // head_dim
    query_heads = query_rows.reshape(row_count, slot_count, head_dim)
    mixture = pl.pallas_call(
        functools.partial(attend_kernel, HEADS // KV_HEADS),
        grid=(unit_count, row_count),
        out_shape=jax.ShapeDtypeStruct((row_count, slot_count, head_dim), jnp.float32),
        in_specs=[
            pl.BlockSpec(memory_space=pltpu.SMEM),
            pl.BlockSpec((row_count, slot_count, head_dim), lambda u, r: (0, 0, 0)),
            pl.BlockSpec((None, None, context, head_dim), lambda u, r: (u, r, 0, 0)),
            pl.BlockSpec((None, None, context, head_dim), lambda u, r: (u, r, 0, 1)),
        ],
        out_specs=pl.BlockSpec((row_count, slot_count, head_dim), lambda u, r: (0, 0, 0)),
        cost_estimate=pl.CostEstimate(
            flops=4 * cache_units.size * slot_count // 2,
            bytes_accessed=2 * cache_units.size,
            transcendentals=unit_count * row_count * slot_count * context,
        ),
        compiler_params=pltpu.CompilerParams(vmem_limit_bytes=32 * 1024 * 1024),
    )(lengths, query_heads, cache_units, cache_units)
    return mixture.astype(jnp.bfloat16).reshape(row_count, slot_count * head_dim)


def project_layers(flat_heads, weight, layer_of, head_dim):
    lane_layer = jnp.repeat(layer_of, head_dim)
    blank = jnp.zeros_like(flat_heads)
    masked = jnp.stack(
        [jnp.where(lane_layer[None, :] == layer_pos, flat_heads, blank) for layer_pos in (0, 1)]
    )
    return jnp.einsum("jrs,sd->jrd", masked, weight, preferred_element_type=jnp.float32)


def per_device(
    queries, resident_kv, row_lengths, out_weight, outgoing_kv, block_order, sent_length
):
    second = lax.axis_index("inst") == 1
    parity = lax.axis_index("tensor") % 2
    query_rows = queries[0, 0, 0]
    cache_units = resident_kv[0, 0, 0]
    head_dim = cache_units.shape[-1] // 2
    slot_count = query_rows.shape[1] // head_dim
    per_layer = slot_count // 2
    group_size = HEADS // KV_HEADS
    paired = slot_count > group_size
    slot_ids = jnp.arange(slot_count, dtype=jnp.int32)
    layer_of = jnp.where(second, slot_ids // per_layer, parity)
    stored = outgoing_kv[0, 0, 0]
    unit_count, block_count, block_len, lane_width = stored.shape
    block_ids = block_order[0, 0, 0]
    starts, counts = cuts(block_count)
    chunks = list(first_chunks(stored, block_ids, paired, starts[0], counts[0]))
    chunks += ordered_chunks(stored, block_ids, sent_length, paired, starts[1:], counts[1:])
    arrived = room((unit_count, block_count * block_len, lane_width), stored.dtype)
    landed = [None] * len(chunks)

    def send(parts):
        for part in parts:
            landed[2 * part] = crossed(chunks[2 * part], 0, True)
            landed[2 * part + 1] = crossed(chunks[2 * part + 1], 1, paired)

    early = len(counts) - 2
    send(range(early))
    query_rows, cache_units, landed[2], landed[3] = lax.optimization_barrier(
        (query_rows, cache_units, landed[2], landed[3])
    )
    flat_heads = attend_slots(query_rows, cache_units, row_lengths)
    partial_value = project_layers(flat_heads, out_weight[0, 0, 0], layer_of, head_dim)
    totals = halved_sum(partial_value, "tensor")
    totals, *chunks[2 * early :] = lax.optimization_barrier((totals, *chunks[2 * early :]))
    send(range(early, len(counts)))
    slots = landing_slots(paired)
    last = []
    for part, start in enumerate(starts):
        for way in range(2):
            piece = landed[2 * part + way]
            if 2 * part + way >= len(landed) - 3:
                last.append((piece, (start * block_len, way)))
            else:
                place = (slots[way], start * block_len, 0)
                arrived = lax.dynamic_update_slice(arrived, piece[None], place)
    arrived = place_last(arrived, [piece for piece, _ in last], [at for _, at in last], paired)
    return (totals[None], arrived[None, None, None])


def solution(mesh):
    placed = (
        P("inst", "section", "tensor", None, None),
        P("inst", "section", "tensor", None, None, None, None),
        P("inst", None),
        P("inst", "section", "tensor", None, None),
        P("inst", "section", "tensor", None, None, None, None),
        P("inst", "section", "tensor", None),
        P("inst"),
    )
    return jax.shard_map(
        per_device,
        mesh=mesh,
        in_specs=placed,
        out_specs=(
            P("inst", "section", None, "tensor"),
            P("inst", "section", "tensor", None, None, None),
        ),
        check_vma=False,
    )
```

```python
import functools

import jax
import jax.numpy as jnp
from jax import lax
from jax.experimental import pallas as pl
from jax.experimental.pallas import tpu as pltpu
from jax.sharding import PartitionSpec as P

HEADS = 32
KV_HEADS = 8
SHARES = (4, 5, 9, 8, 5, 1)


def halved_sum(value, axis):
    size = lax.axis_size(axis)
    place = lax.axis_index(axis)
    bit = size.bit_length() - 2
    while bit >= 0:
        step = 1 << bit
        half = value.shape[-1] // 2
        side = (place // step) % 2
        kept = lax.dynamic_slice_in_dim(value, side * half, half, value.ndim - 1)
        given = lax.dynamic_slice_in_dim(value, (1 - side) * half, half, value.ndim - 1)
        value = kept + lax.ppermute(given, axis, [(i, i ^ step) for i in range(size)])
        bit -= 1
    return value


def sent_units(paired):
    parity = lax.axis_index("tensor") % 2
    if paired:
        return parity, 1 - parity
    return lax.axis_index("inst") * parity, 0 * parity


def order_kernel(starts, paired, order_ref, length_ref, stored_ref, *rest):
    chunk_refs, (held, edge, blank, edge_sem, sem) = rest[:-5], rest[-5:]
    block_len = edge.shape[1]
    units = sent_units(paired)
    fetches = []
    for way in range(2):
        fetches.append(
            pltpu.make_async_copy(stored_ref.at[units[way]], held.at[way], edge_sem.at[way])
        )
        fetches[way].start()
    length = length_ref[0]
    full = length // block_len
    blank[...] = jnp.zeros_like(blank)
    for fetch in fetches:
        fetch.wait()

    for part, start in enumerate(starts):
        count = chunk_refs[2 * part].shape[0] // block_len
        whole = jnp.clip(full - start, 0, count)

        def copy_block(i, carry):
            stored_at = order_ref[start + i]
            for way in range(2):
                pltpu.make_async_copy(
                    held.at[way, stored_at],
                    chunk_refs[2 * part + way].at[pl.ds(i * block_len, block_len)],
                    sem,
                ).start()
            return carry

        def blank_block(i, carry):
            for way in range(2):
                pltpu.make_async_copy(
                    blank, chunk_refs[2 * part + way].at[pl.ds(i * block_len, block_len)], sem
                ).start()
            return carry

        lax.fori_loop(0, whole, copy_block, 0)
        here = (full >= start) & (full < start + count)

        @pl.when(here)
        def _():
            stored_at = order_ref[full]
            rows = lax.broadcasted_iota(jnp.int32, edge.shape, 1)
            edge[...] = jnp.where(
                rows < length - full * block_len, held[:, stored_at].astype(jnp.float32), 0.0
            ).astype(edge.dtype)
            for way in range(2):
                pltpu.make_async_copy(
                    edge.at[way],
                    chunk_refs[2 * part + way].at[pl.ds((full - start) * block_len, block_len)],
                    sem,
                ).start()

        lax.fori_loop(whole + here.astype(jnp.int32), count, blank_block, 0)

    for chunk_ref in chunk_refs:
        pltpu.make_async_copy(chunk_ref, chunk_ref, sem).wait()


def first_kernel(paired, order_ref, stored_ref, same_ref, other_ref, sem):
    block_len = stored_ref.shape[2]
    units = sent_units(paired)
    for i in range(same_ref.shape[0] // block_len):
        for unit, chunk_ref in zip(units, (same_ref, other_ref)):
            pltpu.make_async_copy(
                stored_ref.at[unit, order_ref[i]], chunk_ref.at[pl.ds(i * block_len, block_len)], sem
            ).start()
    for chunk_ref in (same_ref, other_ref):
        pltpu.make_async_copy(chunk_ref, chunk_ref, sem).wait()


def first_chunks(stored, block_ids, paired, count):
    block_len, lane_width = stored.shape[2:]
    chunk_shape = jax.ShapeDtypeStruct((count * block_len, lane_width), stored.dtype)
    return pl.pallas_call(
        functools.partial(first_kernel, paired),
        out_shape=[chunk_shape] * 2,
        in_specs=[
            pl.BlockSpec(memory_space=pltpu.SMEM),
            pl.BlockSpec(memory_space=pltpu.HBM),
        ],
        out_specs=[pl.BlockSpec(memory_space=pltpu.VMEM)] * 2,
        scratch_shapes=[pltpu.SemaphoreType.DMA],
        compiler_params=pltpu.CompilerParams(vmem_limit_bytes=60 * 1024 * 1024),
    )(block_ids, stored)


def room_kernel(out_ref):
    pass


def room(shape, dtype):
    return pl.pallas_call(
        room_kernel,
        out_shape=jax.ShapeDtypeStruct(shape, dtype),
        out_specs=pl.BlockSpec(memory_space=pltpu.HBM),
    )()


def ordered_chunks(stored, block_ids, sent_length, paired, starts, counts):
    block_len, lane_width = stored.shape[2:]
    chunk_shapes = []
    for count in counts:
        chunk_shapes += [jax.ShapeDtypeStruct((count * block_len, lane_width), stored.dtype)] * 2
    total = sum(counts) * block_len * lane_width * 2
    return pl.pallas_call(
        functools.partial(order_kernel, starts, paired),
        out_shape=chunk_shapes,
        in_specs=[
            pl.BlockSpec(memory_space=pltpu.SMEM),
            pl.BlockSpec(memory_space=pltpu.SMEM),
            pl.BlockSpec(memory_space=pltpu.HBM),
        ],
        out_specs=[pl.BlockSpec(memory_space=pltpu.HBM)] * len(chunk_shapes),
        scratch_shapes=[
            pltpu.VMEM((2,) + stored.shape[1:], stored.dtype),
            pltpu.VMEM((2, block_len, lane_width), stored.dtype),
            pltpu.VMEM((block_len, lane_width), stored.dtype),
            pltpu.SemaphoreType.DMA((2,)),
            pltpu.SemaphoreType.DMA,
        ],
        compiler_params=pltpu.CompilerParams(vmem_limit_bytes=48 * 1024 * 1024),
        cost_estimate=pl.CostEstimate(flops=0, bytes_accessed=4 * total, transcendentals=0),
    )(block_ids, sent_length, stored)


def cuts(block_count):
    unit = block_count // 32
    counts = [share * unit for share in SHARES]
    starts = [sum(counts[:i]) for i in range(len(counts))]
    return starts, counts


def crossed(chunk, flip, both):
    size = lax.axis_size("tensor")
    route = [(t, size + (t ^ flip)) for t in range(size)]
    if both:
        route += [(size + t, t ^ flip) for t in range(size)]
    return lax.ppermute(chunk, ("inst", "tensor"), route)


def attend_kernel(group_size, lengths_ref, query_ref, keys_ref, values_ref, out_ref):
    unit, row = pl.program_id(0), pl.program_id(1)
    slot_count, head_dim = query_ref.shape[1:]
    context = keys_ref.shape[0]
    scores = lax.dot_general(
        query_ref[row], keys_ref[...], (((1,), (1,)), ((), ())), preferred_element_type=jnp.float32
    ) * head_dim ** (-0.5)
    positions = lax.broadcasted_iota(jnp.int32, (slot_count, context), 1)
    scores = jnp.where(positions < lengths_ref[0, row], scores, -1e30)
    raised = jnp.exp(scores - jnp.max(scores, axis=1, keepdims=True))
    weights = (raised / jnp.sum(raised, axis=1, keepdims=True)).astype(jnp.bfloat16)
    mixture = jnp.dot(weights, values_ref[...], preferred_element_type=jnp.float32)
    slot_ids = lax.broadcasted_iota(jnp.int32, (slot_count, head_dim), 0)
    second = lax.axis_index("inst") == 1
    beyond = jnp.where(second, slot_count // 2, group_size)
    mine = (slot_ids >= beyond) == (unit == 1)

    @pl.when(unit == 0)
    def _():
        out_ref[row] = mixture

    @pl.when(unit == 1)
    def _():
        out_ref[row] = jnp.where(mine, mixture, out_ref[row])


def attend_slots(query_rows, cache_units, lengths):
    row_count = query_rows.shape[0]
    unit_count, _, context, lane_width = cache_units.shape
    head_dim = lane_width // 2
    slot_count = query_rows.shape[1] // head_dim
    query_heads = query_rows.reshape(row_count, slot_count, head_dim)
    mixture = pl.pallas_call(
        functools.partial(attend_kernel, HEADS // KV_HEADS),
        grid=(unit_count, row_count),
        out_shape=jax.ShapeDtypeStruct((row_count, slot_count, head_dim), jnp.float32),
        in_specs=[
            pl.BlockSpec(memory_space=pltpu.SMEM),
            pl.BlockSpec((row_count, slot_count, head_dim), lambda u, r: (0, 0, 0)),
            pl.BlockSpec((None, None, context, head_dim), lambda u, r: (u, r, 0, 0)),
            pl.BlockSpec((None, None, context, head_dim), lambda u, r: (u, r, 0, 1)),
        ],
        out_specs=pl.BlockSpec((row_count, slot_count, head_dim), lambda u, r: (0, 0, 0)),
        cost_estimate=pl.CostEstimate(
            flops=4 * cache_units.size * slot_count // 2,
            bytes_accessed=2 * cache_units.size,
            transcendentals=unit_count * row_count * slot_count * context,
        ),
        compiler_params=pltpu.CompilerParams(vmem_limit_bytes=32 * 1024 * 1024),
    )(lengths, query_heads, cache_units, cache_units)
    return mixture.astype(jnp.bfloat16).reshape(row_count, slot_count * head_dim)


def project_layers(flat_heads, weight, layer_of, head_dim):
    lane_layer = jnp.repeat(layer_of, head_dim)
    blank = jnp.zeros_like(flat_heads)
    masked = jnp.stack(
        [jnp.where(lane_layer[None, :] == layer_pos, flat_heads, blank) for layer_pos in (0, 1)]
    )
    return jnp.einsum("jrs,sd->jrd", masked, weight, preferred_element_type=jnp.float32)


def per_device(
    queries, resident_kv, row_lengths, out_weight, outgoing_kv, block_order, sent_length
):
    second = lax.axis_index("inst") == 1
    parity = lax.axis_index("tensor") % 2
    query_rows = queries[0, 0, 0]
    cache_units = resident_kv[0, 0, 0]
    head_dim = cache_units.shape[-1] // 2
    slot_count = query_rows.shape[1] // head_dim
    per_layer = slot_count // 2
    group_size = HEADS // KV_HEADS
    paired = slot_count > group_size
    slot_ids = jnp.arange(slot_count, dtype=jnp.int32)
    layer_of = jnp.where(second, slot_ids // per_layer, parity)
    stored = outgoing_kv[0, 0, 0]
    unit_count, block_count, block_len, lane_width = stored.shape
    block_ids = block_order[0, 0, 0]
    starts, counts = cuts(block_count)
    chunks = list(first_chunks(stored, block_ids, paired, counts[0]))
    chunks += ordered_chunks(stored, block_ids, sent_length, paired, starts[1:], counts[1:])
    if paired:
        same_slot, other_slot = parity, 1 - parity
    else:
        same_slot = jnp.where(second, parity, 0)
        other_slot = jnp.where(second, 1 - parity, 1)
    arrived = room((unit_count, block_count * block_len, lane_width), stored.dtype)
    landed = [None] * len(chunks)

    def send(parts):
        for part in parts:
            landed[2 * part] = crossed(chunks[2 * part], 0, True)
            landed[2 * part + 1] = crossed(chunks[2 * part + 1], 1, paired)

    early = len(counts) - 2
    send(range(early))
    query_rows, cache_units, landed[2], landed[3] = lax.optimization_barrier(
        (query_rows, cache_units, landed[2], landed[3])
    )
    flat_heads = attend_slots(query_rows, cache_units, row_lengths)
    partial_value = project_layers(flat_heads, out_weight[0, 0, 0], layer_of, head_dim)
    totals = halved_sum(partial_value, "tensor")
    totals, *chunks[2 * early :] = lax.optimization_barrier((totals, *chunks[2 * early :]))
    send(range(early, len(counts)))
    for part, start in enumerate(starts):
        for way, slot in enumerate((same_slot, other_slot)):
            place = (slot, start * block_len, 0)
            arrived = lax.dynamic_update_slice(arrived, landed[2 * part + way][None], place)
    return (totals[None], arrived[None, None, None])


def solution(mesh):
    placed = (
        P("inst", "section", "tensor", None, None),
        P("inst", "section", "tensor", None, None, None, None),
        P("inst", None),
        P("inst", "section", "tensor", None, None),
        P("inst", "section", "tensor", None, None, None, None),
        P("inst", "section", "tensor", None),
        P("inst"),
    )
    return jax.shard_map(
        per_device,
        mesh=mesh,
        in_specs=placed,
        out_specs=(
            P("inst", "section", None, "tensor"),
            P("inst", "section", "tensor", None, None, None),
        ),
        check_vma=False,
    )
```
